32 devices in a mesh: row: 4 (over z), inst: 8 (over y, x, core).
Axes of the slice: x: 2, y: 2, z: 4, core: 2. Of those that a mesh axis runs over, the one named last changes fastest.
Arguments:
- design: bfloat16 [8192, 16384], P('row', 'inst'), may hold values from -0.046875 to 0.046875
- labels: int32 [8192, 256], P('row'), may hold values 0 or 1
- saved_logits: float32 [3, 8192, 256], P(None, 'row'), may hold values from -8 to 8
- saved_coefficients: bfloat16 [3, 16384, 256], P(None, 'inst'), may hold values from -6 to 6
- cotangent: float32 [16384, 256], P('inst'), may hold values from -2 to 2
Outputs:
- first_adjoint: float32 [16384, 256], P('inst')
- design_grad: float32 [8192, 16384], P('row', 'inst')
The draws below stay inside these ranges and needn't reach their ends.
All inputs are finite; a program needn't handle non-finite values. No bound on the sum of `labels` on one device may be relied on, other than what follows from the above.
Results may differ from the reference program's by a relative error of at most 0.0026.
Values may be sent and summed in bfloat16 or wider, within the bound.
No kernel may reach another device: no remote copies, remote signals or barrier semaphores. Data moves between devices by JAX's collectives and lax.ppermute only.
A program may use at most 192 MiB of HBM per device.

```python
import jax
import jax.numpy as jnp

P_SIZE = 16384
K = 256
STEPS = 3
N = 8192


def place_ends(result, rng, smallest, top_value):
    place = [jax.random.randint(jax.random.fold_in(rng, axis), (), 0, length) for axis, length in enumerate(result.shape)]
    widest = result.shape.index(max(result.shape))
    neighbour = place[:widest] + [(place[widest] + 1) % result.shape[widest]] + place[widest + 1:]
    return result.at[tuple(place)].set(smallest).at[tuple(neighbour)].set(top_value)


def level_of(rng, dims, pieces, least, top_value):
    def one(axis_at, blocks):
        heights = jax.random.uniform(jax.random.fold_in(jax.random.fold_in(rng, 6), axis_at), (blocks,), jnp.float32, least / len(pieces), top_value / len(pieces))
        return jnp.repeat(jnp.exp(heights), dims[axis_at] // blocks).reshape((-1,) + (1,) * (len(dims) - axis_at - 1))

    loudness = one(*pieces[0])
    for cut in pieces[1:]:
        loudness = loudness * one(*cut)
    return loudness


def normal_values(own_key, shape, scale, limit, split=(), held_as=jnp.bfloat16):
    drawn = jax.random.normal(own_key, shape, jnp.float32) * scale
    if len(split) > 0:
        drawn = level_of(own_key, shape, split, -0.22, 0.18) * drawn
    return jnp.clip(drawn, min=-limit, max=limit).astype(held_as)


def setup_inputs(seed: int = 0) -> dict:
    arg_keys = jax.random.split(jax.random.key(seed), 6)
    design = normal_values(arg_keys[0], (N, P_SIZE), P_SIZE ** -0.5, 0.046875, ((0, 4), (1, 8)))
    labels = place_ends((jax.random.randint(arg_keys[1], (N, K), 0, 2) < 1).astype(jnp.int32), jax.random.fold_in(arg_keys[1], 1), 0, 1)
    saved_logits = normal_values(arg_keys[2], (STEPS, N, K), 2.0, 8.0, ((1, 4),), jnp.float32)
    saved_coefficients = normal_values(arg_keys[3], (STEPS, P_SIZE, K), 1.0, 6.0, ((1, 8),))
    cotangent = normal_values(arg_keys[4], (P_SIZE, K), 0.25, 2.0, ((0, 8),), jnp.float32)
    return dict(design=design, labels=labels, saved_logits=saved_logits, saved_coefficients=saved_coefficients, cotangent=cotangent)


def reference(design, labels, saved_logits, saved_coefficients, cotangent):
    step_rate = 2.0
    adjoint = cotangent
    accum = jnp.zeros((design.shape[0], design.shape[1]), jnp.float32)
    targets = labels.astype(jnp.float32)
    for step in range(STEPS - 1, -1, -1):
        adjoint_low = adjoint.astype(jnp.bfloat16)
        product = jnp.dot(design, adjoint_low, preferred_element_type=jnp.float32)
        probability = jax.nn.sigmoid(saved_logits[step])
        curvature = probability * (1.0 - probability)
        residual = (probability - targets).astype(jnp.bfloat16)
        weighted = (curvature * product).astype(jnp.bfloat16)
        hessian_term = jnp.dot(design.T, weighted, preferred_element_type=jnp.float32)
        accum = accum + jnp.dot(residual, adjoint_low.T, preferred_element_type=jnp.float32)
        accum = accum + jnp.dot(weighted, saved_coefficients[step].T, preferred_element_type=jnp.float32)
        adjoint = adjoint - step_rate * hessian_term
    return adjoint, -step_rate * accum
```

```python
import functools

import jax
import jax.numpy as jnp
from jax import lax
from jax.experimental import pallas as pl
from jax.experimental.pallas import tpu as pltpu
from jax.sharding import PartitionSpec as P

RATE = 2.0
CHAINS = 2
PIECES = 2
F32 = jnp.float32
BF16 = jnp.bfloat16
VMEM = pl.BlockSpec(memory_space=pltpu.VMEM)
SMEM = pl.BlockSpec(memory_space=pltpu.SMEM)


def cost(flops, nbytes):
    return pl.CostEstimate(flops=flops, bytes_accessed=nbytes, transcendentals=0)


def forward_kernel(core, z, low, keep, send):
    half = keep.shape[0]
    own = pl.multiple_of(core[0] * half, half)
    other = pl.multiple_of((1 - core[0]) * half, half)
    send[...] = jnp.dot(z[pl.ds(other, half), :], low[...], preferred_element_type=F32).astype(BF16)
    keep[...] = jnp.dot(z[pl.ds(own, half), :], low[...], preferred_element_type=F32)


def forward(core, z, low):
    half, cols = z.shape[0] // 2, low.shape[1]
    return pl.pallas_call(
        forward_kernel,
        in_specs=[SMEM, VMEM, VMEM],
        out_specs=[VMEM, VMEM],
        out_shape=[jax.ShapeDtypeStruct((half, cols), F32), jax.ShapeDtypeStruct((half, cols), BF16)],
        compiler_params=pltpu.CompilerParams(vmem_limit_bytes=14 << 20),
        cost_estimate=cost(2 * z.shape[0] * z.shape[1] * 256, 1 << 20),
        name="forward",
    )(core, z, low)


def backward_kernel(piece, core, z, w_own, w_other, out):
    half, width = w_own.shape[0], out.shape[0]
    own = pl.multiple_of(core[0] * half, half)
    other = pl.multiple_of((1 - core[0]) * half, half)
    cols = pl.ds(piece * width, width)
    dims = (((0,), (0,)), ((), ()))
    total = lax.dot_general(w_own[...], z[pl.ds(own, half), cols], dims, preferred_element_type=F32)
    total += lax.dot_general(w_other[...], z[pl.ds(other, half), cols], dims, preferred_element_type=F32)
    out[...] = total.T.astype(BF16)


def backward(core, z, w_own, w_other, piece, pieces):
    width = z.shape[1] // pieces
    return pl.pallas_call(
        functools.partial(backward_kernel, piece),
        in_specs=[SMEM, VMEM, VMEM, VMEM],
        out_specs=VMEM,
        out_shape=jax.ShapeDtypeStruct((width, w_own.shape[1]), BF16),
        compiler_params=pltpu.CompilerParams(vmem_limit_bytes=14 << 20),
        cost_estimate=cost(2 * z.shape[0] * width * 256, 1 << 20),
        name="backward",
    )(core, z, w_own, w_other)


def outer_kernel(count, *refs):
    left, right, out = refs[:count], refs[count : 2 * count], refs[2 * count]
    dims = (((1,), (1,)), ((), ()))
    total = lax.dot_general(left[0][...], right[0][...], dims, preferred_element_type=F32)
    for a, b in zip(left[1:], right[1:]):
        total += lax.dot_general(a[...], b[...], dims, preferred_element_type=F32)
    out[...] = -RATE * total


def outer(left, right):
    rows, depth = left[0].shape
    cols = right[0].shape[0]
    block = min(256, rows)
    return pl.pallas_call(
        functools.partial(outer_kernel, len(left)),
        grid=(rows // block,),
        in_specs=[pl.BlockSpec((block, depth), lambda i: (i, 0)) for _ in left] + [VMEM for _ in right],
        out_specs=pl.BlockSpec((block, cols), lambda i: (i, 0)),
        out_shape=jax.ShapeDtypeStruct((rows, cols), F32),
        compiler_params=pltpu.CompilerParams(vmem_limit_bytes=30 << 20),
        cost_estimate=cost(2 * rows * cols * depth * len(left), rows * cols * 4),
        name="outer",
    )(*left, *right)


def sum_inst(keep, send, count):
    bits = [1 << b for b in range(1, count.bit_length() - 1)]
    total = keep + lax.ppermute(send, "inst", [(i, i ^ 1) for i in range(count)]).astype(F32)
    for step in range(len(bits)):
        order = (bits[step], bits[(step + 1) % len(bits)])
        pairs = [(i, i ^ order[i & 1]) for i in range(count)]
        total = total + lax.ppermute(total.astype(BF16), "inst", pairs).astype(F32)
    return total


def sum_row(parts, place, count):
    middle = count // 2
    for hop in range(middle - 1):
        pairs = [(hop, hop + 1), (count - 1 - hop, count - 2 - hop)]
        parts = [
            (p.astype(F32) + lax.ppermute(p, "row", pairs).astype(F32)).astype(BF16) for p in parts
        ]
    pairs = [(middle - 1, middle), (middle, middle - 1)]
    parts = [(p.astype(F32) + lax.ppermute(p, "row", pairs).astype(F32)).astype(BF16) for p in parts]
    for hop in range(middle - 1, 0, -1):
        pairs = [(hop, hop - 1), (count - 1 - hop, count - hop)]
        takes = (place == hop - 1) | (place == count - hop)
        parts = [jnp.where(takes, lax.ppermute(p, "row", pairs), p) for p in parts]
    return parts


def shards(rows_count, inst_count, design, labels, saved_logits, saved_coefficients, cotangent):
    steps, rows, depth = saved_logits.shape
    half, cols = rows // 2, depth // CHAINS
    width = design.shape[1] // PIECES
    core = lax.axis_index("inst") % 2
    place = lax.axis_index("row")
    core_ref = core.astype(jnp.int32).reshape(1)
    swap = [(i, i ^ 1) for i in range(inst_count)]
    targets = labels.astype(F32)
    adjoint = [
        [cotangent[p * width : (p + 1) * width, c * cols : (c + 1) * cols] for p in range(PIECES)]
        for c in range(CHAINS)
    ]
    left, right = [], []
    for step in range(steps - 1, -1, -1):
        residual = (jax.nn.sigmoid(saved_logits[step]) - targets).astype(BF16)
        lows, weights = [], []
        for c in range(CHAINS):
            low = jnp.concatenate([p.astype(BF16) for p in adjoint[c]], axis=0)
            keep, send = forward(core_ref, design, low)
            product = sum_inst(keep, send, inst_count)
            logits = lax.dynamic_slice(
                saved_logits, (step, core * half, c * cols), (1, half, cols)
            )[0]
            probability = jax.nn.sigmoid(logits)
            w_own = (probability * (1.0 - probability) * product).astype(BF16)
            w_other = lax.ppermute(w_own, "inst", swap)
            hessian = [
                backward(core_ref, design, w_own, w_other, p, PIECES) for p in range(PIECES)
            ]
            hessian = sum_row(hessian, place, rows_count)
            adjoint[c] = [a - RATE * h.astype(F32) for a, h in zip(adjoint[c], hessian)]
            lows.append(low)
            weights.append(
                jnp.where(
                    core == 0,
                    jnp.concatenate([w_own, w_other], axis=0),
                    jnp.concatenate([w_other, w_own], axis=0),
                )
            )
        left += [residual, jnp.concatenate(weights, axis=1)]
        right += [jnp.concatenate(lows, axis=1), saved_coefficients[step]]
    first = jnp.concatenate([jnp.concatenate(a, axis=0) for a in adjoint], axis=1)
    return first, outer(left, right)


def solution(mesh):
    placed = (
        P("row", "inst"),
        P("row", None),
        P(None, "row", None),
        P(None, "inst", None),
        P("inst", None),
    )
    return jax.shard_map(
        functools.partial(shards, mesh.shape["row"], mesh.shape["inst"]),
        mesh=mesh,
        in_specs=placed,
        out_specs=(P("inst", None), P("row", "inst")),
        check_vma=False,
    )
```

```python
import functools

import jax
import jax.numpy as jnp
from jax import lax
from jax.experimental import pallas as pl
from jax.experimental.pallas import tpu as pltpu
from jax.sharding import PartitionSpec as P

RATE = 2.0
PARTS = 4
F32 = jnp.float32
BF16 = jnp.bfloat16
ANY = pl.BlockSpec(memory_space=pl.ANY)
VMEM = pl.BlockSpec(memory_space=pltpu.VMEM)
SMEM = pl.BlockSpec(memory_space=pltpu.SMEM)
FREE = pl.CostEstimate(flops=0, bytes_accessed=0, transcendentals=0)


def span(bit, size):
    return pl.ds(pl.multiple_of(bit * size, size), size)


def near(value):
    return pltpu.with_memory_space_constraint(value, pltpu.VMEM)


def call(body, outs, *operands, name, scratch=(), limit=12):
    return pl.pallas_call(
        body,
        in_specs=[SMEM] + [VMEM] * (len(operands) - 1),
        out_specs=[VMEM] * len(outs),
        out_shape=[pltpu.VMEM(shape, dtype) for shape, dtype in outs],
        scratch_shapes=[pltpu.VMEM(shape, dtype) for shape, dtype in scratch],
        compiler_params=pltpu.CompilerParams(vmem_limit_bytes=limit << 20),
        cost_estimate=FREE,
        name=name,
    )(operands[0], *[near(v) for v in operands[1:]])


def hold_kernel(source, *refs):
    out, sem = refs[-2:]
    copy = pltpu.make_async_copy(source, out, sem)
    copy.start()
    copy.wait()


def hold(z, *others):
    return pl.pallas_call(
        hold_kernel,
        in_specs=[pl.BlockSpec(memory_space=pltpu.HBM)] + [ANY for _ in others],
        out_specs=VMEM,
        out_shape=pltpu.VMEM(z.shape, z.dtype),
        scratch_shapes=[pltpu.SemaphoreType.DMA],
        compiler_params=pltpu.CompilerParams(vmem_limit_bytes=10 << 20),
        cost_estimate=FREE,
        name="hold",
    )(pltpu.with_memory_space_constraint(z, pltpu.HBM), *others)


def prepare_kernel(halves, index, logits, labels, residual, *curvatures):
    probability = jax.nn.sigmoid(logits[0])
    residual[...] = (probability - labels[...].astype(F32)).astype(BF16)

    @pl.when(pl.program_id(0) < halves)
    def _():
        cols = curvatures[0].shape[1]
        for c, curvature in enumerate(curvatures):
            mine = probability[:, c * cols : (c + 1) * cols]
            curvature[...] = mine * (1.0 - mine)


def prepare(index, logits, labels, step):
    _, rows, depth = logits.shape
    block = min(256, rows // 2)
    count = rows // block
    place = lambda i, index: ((i + index[0] * (count // 2)) % count, 0)
    own = pl.BlockSpec((block, depth // 2), lambda i, index: (jnp.minimum(i, count // 2 - 1), 0))
    return pl.pallas_call(
        functools.partial(prepare_kernel, count // 2),
        grid_spec=pltpu.PrefetchScalarGridSpec(
            num_scalar_prefetch=1,
            grid=(count,),
            in_specs=[
                pl.BlockSpec((1, block, depth), lambda i, index: (step, *place(i, index))),
                pl.BlockSpec((block, depth), place),
            ],
            out_specs=[pl.BlockSpec((block, depth), place), own, own],
        ),
        out_shape=[jax.ShapeDtypeStruct((rows, depth), BF16)]
        + [jax.ShapeDtypeStruct((rows // 2, depth // 2), F32)] * 2,
        compiler_params=pltpu.CompilerParams(vmem_limit_bytes=12 << 20),
        cost_estimate=FREE,
        name="prepare",
    )(index, logits, labels)


def part_out(index, which, total, kept, sent):
    half = kept.shape[0]
    sent[...] = total[span(1 - index[which], half), :].astype(BF16)
    kept[...] = total[span(index[which], half), :]


def first_kernel(start, out):
    out[...] = start[...]


def columns(start, c):
    count, depth = start.shape
    return pl.pallas_call(
        first_kernel,
        grid=(1,),
        in_specs=[pl.BlockSpec((count, depth // 2), lambda i: (0, c))],
        out_specs=pl.BlockSpec((count, depth // 2), lambda i: (0, 0)),
        out_shape=jax.ShapeDtypeStruct((count, depth // 2), F32),
        compiler_params=pltpu.CompilerParams(vmem_limit_bytes=12 << 20),
        cost_estimate=FREE,
        name="columns",
    )(start)


def forward_kernel(updates, index, z, adjoint, *refs):
    hessian, (*new, low, kept, sent, total) = refs[:updates], refs[updates:]
    if updates:
        half = hessian[0].shape[0]
        for bit, h in zip((index[1], 1 - index[1]), hessian):
            rows = span(bit, half)
            value = adjoint[rows, :] - RATE * h[...].astype(F32)
            new[0][rows, :] = value
            low[rows, :] = value.astype(BF16)
    else:
        low[...] = adjoint[...].astype(BF16)
    total[...] = jnp.dot(z[...], low[...], preferred_element_type=F32)
    part_out(index, 0, total, kept, sent)


def forward(index, z, adjoint, hessian):
    (rows, width), cols = z.shape, adjoint.shape[1]
    outs = [((width, cols), F32)] if hessian else []
    outs += [((width, cols), BF16), ((rows // 2, cols), F32), ((rows // 2, cols), BF16)]
    body = functools.partial(forward_kernel, len(hessian))
    out = call(body, outs, index, z, adjoint, *hessian, name="forward", scratch=[((rows, cols), F32)])
    return out if hessian else [adjoint, *out]


def add_kernel(index, one, two, total, low):
    value = one[...] + two[...].astype(F32)
    total[...] = value
    low[...] = value.astype(BF16)


def add(index, one, two):
    return call(add_kernel, [(one.shape, F32), (one.shape, BF16)], index, one, two, name="add")


def weigh_kernel(index, one, two, curvature, out):
    out[...] = (curvature[...] * (one[...] + two[...].astype(F32))).astype(BF16)


def weigh(index, one, two, curvature):
    return call(weigh_kernel, [(one.shape, BF16)], index, one, two, curvature, name="weigh")[0]


def backward_kernel(index, z, w_own, w_other, weight, kept, sent, total):
    half = w_own.shape[0]
    weight[span(index[0], half), :] = w_own[...]
    weight[span(1 - index[0], half), :] = w_other[...]
    dims = (((0,), (0,)), ((), ()))
    total[...] = lax.dot_general(weight[...], z[...], dims, preferred_element_type=F32).T
    part_out(index, 1, total, kept, sent)


def backward(index, z, w_own, w_other):
    (rows, width), cols = z.shape, w_own.shape[1]
    outs = [((rows, cols), BF16), ((width // 2, cols), F32), ((width // 2, cols), BF16)]
    return call(
        backward_kernel, outs, index, z, w_own, w_other, name="backward", scratch=[((width, cols), F32)]
    )


def merge_kernel(index, one, two, out):
    out[...] = (one[...].astype(F32) + two[...].astype(F32)).astype(BF16)


def merge(index, one, two):
    return call(merge_kernel, [(one.shape, BF16)], index, one, two, name="merge")[0]


def join_kernel(index, one, two, out):
    cols = one.shape[1]
    out[:, :cols] = one[...]
    out[:, cols:] = two[...]


def join(index, one, two):
    return call(join_kernel, [((one.shape[0], 2 * one.shape[1]), BF16)], index, one, two, name="join")[0]


def finish_kernel(index, adjoint, own, other, *refs):
    out, half = refs[-1], own.shape[0]
    for bit, h in zip((index[1], 1 - index[1]), (own, other)):
        rows = span(bit, half)
        out[rows, :] = adjoint[rows, :] - RATE * h[...].astype(F32)


def finish(index, adjoint, hessian, c, held):
    count, cols = adjoint.shape
    return pl.pallas_call(
        finish_kernel,
        grid=(1,),
        in_specs=[SMEM, VMEM, VMEM, VMEM] + [ANY for _ in held],
        out_specs=pl.BlockSpec((count, cols), lambda i: (0, c)),
        out_shape=jax.ShapeDtypeStruct((count, 2 * cols), F32),
        input_output_aliases={4: 0} if held else {},
        compiler_params=pltpu.CompilerParams(vmem_limit_bytes=12 << 20),
        cost_estimate=FREE,
        name="finish",
    )(index, *[near(v) for v in (adjoint, *hessian)], *held)


def outer_kernel(steps, *refs):
    residuals, weights, lows = refs[:steps], refs[steps : 2 * steps], refs[2 * steps : 3 * steps]
    coefficients, out = refs[3 * steps], refs[-1]
    dims = (((1,), (1,)), ((), ()))
    pairs = [(r[...], b[...]) for r, b in zip(residuals, lows)]
    pairs += [(w[...], coefficients[steps - 1 - k]) for k, w in enumerate(weights)]
    total = lax.dot_general(*pairs[0], dims, preferred_element_type=F32)
    for a, b in pairs[1:]:
        total += lax.dot_general(a, b, dims, preferred_element_type=F32)
    out[...] = -RATE * total


def outer(residuals, weights, lows, coefficients, part, held):
    rows, depth = residuals[0].shape
    steps, cols = coefficients.shape[:2]
    block = min(256, rows // PARTS)
    count = rows // PARTS // block
    first = part * count
    left = [*residuals, *weights]
    return pl.pallas_call(
        functools.partial(outer_kernel, steps),
        grid=(count,),
        in_specs=[pl.BlockSpec((block, depth), lambda i: (first + i, 0)) for _ in left]
        + [VMEM] * (steps + 1)
        + [ANY for _ in held],
        out_specs=pl.BlockSpec((block, cols), lambda i: (first + i, 0)),
        out_shape=jax.ShapeDtypeStruct((rows, cols), F32),
        input_output_aliases={3 * steps + 1: 0} if held else {},
        compiler_params=pltpu.CompilerParams(vmem_limit_bytes=14 << 20),
        cost_estimate=FREE,
        name="outer",
    )(*left, *[near(v) for v in (*lows, coefficients)], *held)


def swap(value, axis, count, bit):
    return lax.ppermute(value, axis, [(i, i ^ bit) for i in range(count)])


class Turn:
    def __init__(self):
        self.last = ()

    def begin(self, *values):
        return lax.optimization_barrier((*values, *self.last))[: len(values)]

    def end(self, value):
        self.last = (value,)


def chain(turn, counts, index, z, curvature, adjoint, steps):
    rows_count, inst_count = counts
    crossings = [1 << b for b in range(1, inst_count.bit_length() - 1)]
    crossings_row = [1 << b for b in range(1, rows_count.bit_length() - 1)]
    hessian = ()
    for step in range(steps - 1, -1, -1):
        adjoint, *hessian = turn.begin(adjoint, *hessian)
        adjoint, low, product, sent = forward(index, z, adjoint, hessian)
        turn.end(product)
        sent = swap(sent, "inst", inst_count, 1)
        yield "V", low
        for k in range(len(crossings)):
            product, sent = turn.begin(product, sent)
            product, moved = add(index, product, sent)
            turn.end(moved)
            bits = (crossings[k], crossings[(k + 1) % len(crossings)])
            sent = lax.ppermute(moved, "inst", [(i, i ^ bits[i & 1]) for i in range(inst_count)])
            yield f"x{k}", None
        product, sent = turn.begin(product, sent)
        w_own = weigh(index, product, sent, curvature[step])
        turn.end(w_own)
        w_other = swap(w_own, "inst", inst_count, 1)
        yield "W", None
        w_own, w_other = turn.begin(w_own, w_other)
        weight, total, sent = backward(index, z, w_own, w_other)
        turn.end(total)
        if rows_count > 1:
            sent = swap(sent, "row", rows_count, 1)
        yield "H", weight
        if rows_count > 1:
            for k in range(len(crossings_row) + 1):
                total, sent = turn.begin(total, sent)
                total = merge(index, total, sent)
                turn.end(total)
                sent = swap(total, "row", rows_count, (crossings_row + [1])[k])
                yield f"z{k}", None
        hessian = (total, sent)
    yield "end", adjoint, hessian


def shards(rows_count, inst_count, design, labels, saved_logits, saved_coefficients, cotangent):
    steps = saved_logits.shape[0]
    core = lax.axis_index("inst") % 2
    side = lax.axis_index("row") % 2
    index = jnp.stack([core, side]).astype(jnp.int32)
    starts = [columns(cotangent, c) for c in range(2)]
    z = hold(design, index)
    turn = Turn()
    prepared = [prepare(index, saved_logits, labels, step) for step in range(steps)]
    residuals = [p[0] for p in prepared[::-1]]
    chains = [
        chain(turn, (rows_count, inst_count), index, z, [p[1 + c] for p in prepared], starts[c], steps)
        for c in range(2)
    ]
    lows, weights = [], []

    def joined(value):
        (one,) = turn.begin(value[0])
        out = join(index, one, value[1])
        turn.end(out)
        return out

    parts, grad, first = 0, (), ()
    crossings = max(rows_count.bit_length() - 1, 0)
    for c in lagged(steps * (3 + max(inst_count.bit_length() - 2, 0) + crossings), LAG):
        stage, *values = next(chains[c])
        if stage == "V" and c:
            lows.append((seen, values[0]))
        elif stage == "V":
            seen = values[0]
        elif stage == "H" and c:
            weights.append((held, values[0]))
            lows[-1], weights[-1] = joined(lows[-1]), joined(weights[-1])
        elif stage == "H":
            held = values[0]
        if len(weights) == steps and parts < PARTS:
            grad = part_of(turn, residuals, weights, lows, saved_coefficients, parts, grad)
            parts += 1
    for c in range(2):
        _, adjoint, hessian = next(chains[c])
        if c == 1:
            while parts < PARTS:
                grad = part_of(turn, residuals, weights, lows, saved_coefficients, parts, grad)
                parts += 1
        adjoint, *hessian = turn.begin(adjoint, *hessian)
        first = (finish(index, adjoint, hessian, c, first),)
        turn.end(first[0])
    return first[0], grad[0]


def part_of(turn, residuals, weights, lows, coefficients, part, grad):
    low, *rest = turn.begin(lows[0], *lows[1:])
    grad = (outer(residuals, weights, [low, *rest], coefficients, part, grad),)
    turn.end(grad[0])
    return grad


LAG = 1


def lagged(total, lag):
    order = []
    for k in range(total + lag):
        order += [0] if k < total else []
        order += [1] if k >= lag else []
    return order


def plain(design, labels, saved_logits, saved_coefficients, cotangent):
    adjoint = cotangent
    accum = jnp.zeros(design.shape, F32)
    targets = labels.astype(F32)
    for step in range(saved_logits.shape[0] - 1, -1, -1):
        low = adjoint.astype(BF16)
        product = lax.psum(jnp.dot(design, low, preferred_element_type=F32), "inst")
        probability = jax.nn.sigmoid(saved_logits[step])
        residual = (probability - targets).astype(BF16)
        weighted = (probability * (1.0 - probability) * product).astype(BF16)
        accum = accum + jnp.dot(residual, low.T, preferred_element_type=F32)
        accum = accum + jnp.dot(weighted, saved_coefficients[step].T, preferred_element_type=F32)
        dims = (((0,), (0,)), ((), ()))
        hessian = lax.dot_general(design, weighted, dims, preferred_element_type=F32)
        adjoint = adjoint - RATE * lax.psum(hessian, "row")
    return adjoint, -RATE * accum


def solution(mesh):
    placed = (
        P("row", "inst"),
        P("row", None),
        P(None, "row", None),
        P(None, "inst", None),
        P("inst", None),
    )
    counts = (mesh.shape["row"], mesh.shape["inst"])
    even = counts[1] > 1 and all(n & (n - 1) == 0 for n in counts)
    return jax.shard_map(
        functools.partial(shards, *counts) if even else plain,
        mesh=mesh,
        in_specs=placed,
        out_specs=(P("inst", None), P("row", "inst")),
        check_vma=False,
    )
```

```python
import functools

import jax
import jax.numpy as jnp
from jax import lax
from jax.experimental import pallas as pl
from jax.experimental.pallas import tpu as pltpu
from jax.sharding import PartitionSpec as P

RATE = 2.0
PARTS = 4
F32 = jnp.float32
BF16 = jnp.bfloat16
ANY = pl.BlockSpec(memory_space=pl.ANY)
VMEM = pl.BlockSpec(memory_space=pltpu.VMEM)
FREE = pl.CostEstimate(flops=0, bytes_accessed=0, transcendentals=0)


def span(bit, size):
    return pl.ds(pl.multiple_of(bit * size, size), size)


def near(value):
    return pltpu.with_memory_space_constraint(value, pltpu.VMEM)


def core_bit():
    return lax.rem(lax.axis_index("inst"), 2)


def side_bit():
    place = lax.axis_index("row")
    return lax.rem(place + lax.div(place, 2), 2)


def call(body, outs, *operands, name, scratch=(), limit=12):
    return pl.pallas_call(
        body,
        in_specs=[VMEM] * len(operands),
        out_specs=[VMEM] * len(outs),
        out_shape=[pltpu.VMEM(shape, dtype) for shape, dtype in outs],
        scratch_shapes=[pltpu.VMEM(shape, dtype) for shape, dtype in scratch],
        compiler_params=pltpu.CompilerParams(vmem_limit_bytes=limit << 20),
        cost_estimate=FREE,
        name=name,
    )(*[near(v) for v in operands])


def prepare_kernel(logits, labels, residual, *curvatures):
    probability = jax.nn.sigmoid(logits[0])
    residual[...] = (probability - labels[...].astype(F32)).astype(BF16)
    cols = curvatures[0].shape[1]
    for c, curvature in enumerate(curvatures):
        mine = probability[:, c * cols : (c + 1) * cols]
        curvature[...] = mine * (1.0 - mine)


def prepare(logits, labels, step):
    _, rows, depth = logits.shape
    block = min(256, rows)
    return pl.pallas_call(
        prepare_kernel,
        grid=(rows // block,),
        in_specs=[
            pl.BlockSpec((1, block, depth), lambda i: (step, i, 0)),
            pl.BlockSpec((block, depth), lambda i: (i, 0)),
        ],
        out_specs=[pl.BlockSpec((block, depth), lambda i: (i, 0))]
        + [pl.BlockSpec((block, depth // 2), lambda i: (i, 0))] * 2,
        out_shape=[jax.ShapeDtypeStruct((rows, depth), BF16)]
        + [jax.ShapeDtypeStruct((rows, depth // 2), F32)] * 2,
        compiler_params=pltpu.CompilerParams(vmem_limit_bytes=12 << 20),
        cost_estimate=FREE,
        name="prepare",
    )(logits, labels)


def part_out(bit, total, kept, sent):
    half = kept.shape[0]
    sent[...] = total[span(1 - bit, half), :].astype(BF16)
    kept[...] = total[span(bit, half), :]


def first_kernel(blocks, source, start, z, adjoint, low, kept, sent, total, sems):
    block = z.shape[0] // blocks
    rows = [pl.ds(k * block, block) for k in range(blocks)]
    copies = [
        pltpu.make_async_copy(source.at[r, :], z.at[r, :], sems.at[k]) for k, r in enumerate(rows)
    ]
    for copy in copies:
        copy.start()
    adjoint[...] = start[...]
    low[...] = start[...].astype(BF16)
    for r, copy in zip(rows, copies):
        copy.wait()
        total[r, :] = jnp.dot(z[r, :], low[...], preferred_element_type=F32)
    part_out(core_bit(), total, kept, sent)


def first_forward(design, start):
    rows, width = design.shape
    cols = start.shape[1] // 2
    blocks = 8
    outs = [((rows, width), BF16), ((width, cols), F32), ((width, cols), BF16)]
    outs += [((rows // 2, cols), F32), ((rows // 2, cols), BF16)]
    return pl.pallas_call(
        functools.partial(first_kernel, blocks),
        grid=(1,),
        in_specs=[
            pl.BlockSpec(memory_space=pltpu.HBM),
            pl.BlockSpec((width, cols), lambda i: (0, 0)),
        ],
        out_specs=[VMEM] * len(outs),
        out_shape=[pltpu.VMEM(shape, dtype) for shape, dtype in outs],
        scratch_shapes=[pltpu.VMEM((rows, cols), F32), pltpu.SemaphoreType.DMA((blocks,))],
        compiler_params=pltpu.CompilerParams(vmem_limit_bytes=16 << 20),
        cost_estimate=FREE,
        name="first",
    )(pltpu.with_memory_space_constraint(design, pltpu.HBM), start)


def columns_kernel(start, out):
    out[...] = start[...]


def columns(start, c):
    count, depth = start.shape
    return pl.pallas_call(
        columns_kernel,
        grid=(1,),
        in_specs=[pl.BlockSpec((count, depth // 2), lambda i: (0, c))],
        out_specs=VMEM,
        out_shape=pltpu.VMEM((count, depth // 2), F32),
        compiler_params=pltpu.CompilerParams(vmem_limit_bytes=12 << 20),
        cost_estimate=FREE,
        name="columns",
    )(start)


def forward_kernel(updates, z, adjoint, *refs):
    hessian, (*new, low, kept, sent, total) = refs[:updates], refs[updates:]
    if updates:
        half = hessian[0].shape[0]
        for bit, h in zip((side_bit(), 1 - side_bit()), hessian):
            rows = span(bit, half)
            value = adjoint[rows, :] - RATE * h[...].astype(F32)
            new[0][rows, :] = value
            low[rows, :] = value.astype(BF16)
    else:
        low[...] = adjoint[...].astype(BF16)
    total[...] = jnp.dot(z[...], low[...], preferred_element_type=F32)
    part_out(core_bit(), total, kept, sent)


def forward(z, adjoint, hessian):
    (rows, width), cols = z.shape, adjoint.shape[1]
    outs = [((width, cols), F32)] if hessian else []
    outs += [((width, cols), BF16), ((rows // 2, cols), F32), ((rows // 2, cols), BF16)]
    body = functools.partial(forward_kernel, len(hessian))
    out = call(body, outs, z, adjoint, *hessian, name="forward", scratch=[((rows, cols), F32)])
    return out if hessian else [adjoint, *out]


def add_kernel(one, two, total, low):
    value = one[...] + two[...].astype(F32)
    total[...] = value
    low[...] = value.astype(BF16)


def add(one, two):
    return call(add_kernel, [(one.shape, F32), (one.shape, BF16)], one, two, name="add")


def weigh_kernel(one, two, curvature, out):
    mine = curvature[span(core_bit(), one.shape[0]), :]
    out[...] = (mine * (one[...] + two[...].astype(F32))).astype(BF16)


def weigh(one, two, curvature):
    return call(weigh_kernel, [(one.shape, BF16)], one, two, curvature, name="weigh")[0]


def backward_kernel(z, w_own, w_other, weight, kept, sent, total):
    half = w_own.shape[0]
    weight[span(core_bit(), half), :] = w_own[...]
    weight[span(1 - core_bit(), half), :] = w_other[...]
    dims = (((0,), (0,)), ((), ()))
    total[...] = lax.dot_general(weight[...], z[...], dims, preferred_element_type=F32).T
    part_out(side_bit(), total, kept, sent)


def backward(z, w_own, w_other):
    (rows, width), cols = z.shape, w_own.shape[1]
    outs = [((rows, cols), BF16), ((width // 2, cols), F32), ((width // 2, cols), BF16)]
    return call(
        backward_kernel, outs, z, w_own, w_other, name="backward", scratch=[((width, cols), F32)]
    )


def merge_kernel(one, two, out):
    out[...] = (one[...].astype(F32) + two[...].astype(F32)).astype(BF16)


def merge(one, two):
    return call(merge_kernel, [(one.shape, BF16)], one, two, name="merge")[0]


def join_kernel(one, two, out):
    cols = one.shape[1]
    out[:, :cols] = one[...]
    out[:, cols:] = two[...]


def join(one, two):
    return call(join_kernel, [((one.shape[0], 2 * one.shape[1]), BF16)], one, two, name="join")[0]


def finish_kernel(adjoint, own, other, *refs):
    out, half = refs[-1], own.shape[0]
    for bit, h in zip((side_bit(), 1 - side_bit()), (own, other)):
        rows = span(bit, half)
        out[rows, :] = adjoint[rows, :] - RATE * h[...].astype(F32)


def finish(adjoint, hessian, c, held):
    count, cols = adjoint.shape
    return pl.pallas_call(
        finish_kernel,
        grid=(1,),
        in_specs=[VMEM, VMEM, VMEM] + [ANY for _ in held],
        out_specs=pl.BlockSpec((count, cols), lambda i: (0, c)),
        out_shape=jax.ShapeDtypeStruct((count, 2 * cols), F32),
        input_output_aliases={3: 0} if held else {},
        compiler_params=pltpu.CompilerParams(vmem_limit_bytes=12 << 20),
        cost_estimate=FREE,
        name="finish",
    )(*[near(v) for v in (adjoint, *hessian)], *held)


def outer_kernel(steps, *refs):
    residuals, weights, lows = refs[:steps], refs[steps : 2 * steps], refs[2 * steps : 3 * steps]
    coefficients, out = refs[3 * steps], refs[-1]
    dims = (((1,), (1,)), ((), ()))
    pairs = [(r[...], b[...]) for r, b in zip(residuals, lows)]
    pairs += [(w[...], coefficients[steps - 1 - k]) for k, w in enumerate(weights)]
    total = lax.dot_general(*pairs[0], dims, preferred_element_type=F32)
    for a, b in pairs[1:]:
        total += lax.dot_general(a, b, dims, preferred_element_type=F32)
    out[...] = -RATE * total


def outer(residuals, weights, lows, coefficients, part, held):
    rows, depth = residuals[0].shape
    steps, cols = coefficients.shape[:2]
    block = min(256, rows // PARTS)
    count = rows // PARTS // block
    first = part * count
    left = [*residuals, *weights]
    return pl.pallas_call(
        functools.partial(outer_kernel, steps),
        grid=(count,),
        in_specs=[pl.BlockSpec((block, depth), lambda i: (first + i, 0)) for _ in left]
        + [VMEM] * (steps + 1)
        + [ANY for _ in held],
        out_specs=pl.BlockSpec((block, cols), lambda i: (first + i, 0)),
        out_shape=jax.ShapeDtypeStruct((rows, cols), F32),
        input_output_aliases={3 * steps + 1: 0} if held else {},
        compiler_params=pltpu.CompilerParams(vmem_limit_bytes=14 << 20),
        cost_estimate=FREE,
        name="outer",
    )(*left, *[near(v) for v in (*lows, coefficients)], *held)


def swap(value, axis, count, bit):
    return lax.ppermute(value, axis, [(i, i ^ bit) for i in range(count)])


class Turn:
    def __init__(self):
        self.last = ()

    def begin(self, *values):
        return lax.optimization_barrier((*values, *self.last))[: len(values)]

    def end(self, value):
        self.last = (value,)


def chain(turn, counts, design, z, curvature, adjoint, steps):
    rows_count, inst_count = counts
    crossings = [1 << b for b in range(1, inst_count.bit_length() - 1)]
    mirrors = [(2 << b) - 1 for b in range(1, rows_count.bit_length() - 1)]
    hessian = ()
    for step in range(steps - 1, -1, -1):
        adjoint, *hessian = turn.begin(adjoint, *hessian)
        if z is None:
            z, adjoint, low, product, sent = first_forward(design, adjoint)
        else:
            adjoint, low, product, sent = forward(z, adjoint, hessian)
        turn.end(product)
        sent = swap(sent, "inst", inst_count, 1)
        yield "V", low, z
        for k in range(len(crossings)):
            product, sent = turn.begin(product, sent)
            product, moved = add(product, sent)
            turn.end(moved)
            bits = (crossings[k], crossings[(k + 1) % len(crossings)])
            sent = lax.ppermute(moved, "inst", [(i, i ^ bits[i & 1]) for i in range(inst_count)])
            yield f"x{k}", None
        product, sent = turn.begin(product, sent)
        w_own = weigh(product, sent, curvature[step])
        turn.end(w_own)
        w_other = swap(w_own, "inst", inst_count, 1)
        yield "W", None
        w_own, w_other = turn.begin(w_own, w_other)
        weight, total, sent = backward(z, w_own, w_other)
        turn.end(total)
        if rows_count > 1:
            sent = swap(sent, "row", rows_count, 1)
        yield "H", weight
        if rows_count > 1:
            for k in range(len(mirrors) + 1):
                total, sent = turn.begin(total, sent)
                total = merge(total, sent)
                turn.end(total)
                sent = swap(total, "row", rows_count, (mirrors + [1])[k])
                yield f"z{k}", None
        hessian = (total, sent)
    yield "end", adjoint, hessian


def shards(rows_count, inst_count, design, labels, saved_logits, saved_coefficients, cotangent):
    steps = saved_logits.shape[0]
    turn = Turn()
    prepared = [prepare(saved_logits, labels, step) for step in range(steps)]
    residuals = [p[0] for p in prepared[::-1]]
    curvatures = [[p[1 + c] for p in prepared] for c in range(2)]
    counts = (rows_count, inst_count)
    chains = [chain(turn, counts, design, None, curvatures[0], cotangent, steps), None]
    lows, weights = [], []

    def joined(value):
        (one,) = turn.begin(value[0])
        out = join(one, value[1])
        turn.end(out)
        return out

    parts, grad, first = 0, (), ()
    crossings = max(rows_count.bit_length() - 1, 0)
    second = columns(cotangent, 1)
    for c in lagged(steps * (3 + max(inst_count.bit_length() - 2, 0) + crossings), LAG):
        if c and chains[1] is None:
            chains[1] = chain(turn, counts, design, z, curvatures[1], second, steps)
        stage, *values = next(chains[c])
        if stage == "V" and c:
            lows.append((seen, values[0]))
        elif stage == "V":
            seen, z = values
        elif stage == "H" and c:
            weights.append((held, values[0]))
            lows[-1], weights[-1] = joined(lows[-1]), joined(weights[-1])
        elif stage == "H":
            held = values[0]
        for _ in range({"H": 1, "z0": 2}.get(stage, 0) if c and len(weights) == steps else 0):
            grad = part_of(turn, residuals, weights, lows, saved_coefficients, parts, grad)
            parts += 1
    for c in range(2):
        _, adjoint, hessian = next(chains[c])
        while c and parts < PARTS:
            grad = part_of(turn, residuals, weights, lows, saved_coefficients, parts, grad)
            parts += 1
        adjoint, *hessian = turn.begin(adjoint, *hessian)
        first = (finish(adjoint, hessian, c, first),)
        turn.end(first[0])
    return first[0], grad[0]


def part_of(turn, residuals, weights, lows, coefficients, part, grad):
    low, *rest = turn.begin(lows[0], *lows[1:])
    grad = (outer(residuals, weights, [low, *rest], coefficients, part, grad),)
    turn.end(grad[0])
    return grad


LAG = 1


def lagged(total, lag):
    order = []
    for k in range(total + lag):
        order += [0] if k < total else []
        order += [1] if k >= lag else []
    return order


def plain(design, labels, saved_logits, saved_coefficients, cotangent):
    adjoint = cotangent
    accum = jnp.zeros(design.shape, F32)
    targets = labels.astype(F32)
    for step in range(saved_logits.shape[0] - 1, -1, -1):
        low = adjoint.astype(BF16)
        product = lax.psum(jnp.dot(design, low, preferred_element_type=F32), "inst")
        probability = jax.nn.sigmoid(saved_logits[step])
        residual = (probability - targets).astype(BF16)
        weighted = (probability * (1.0 - probability) * product).astype(BF16)
        accum = accum + jnp.dot(residual, low.T, preferred_element_type=F32)
        accum = accum + jnp.dot(weighted, saved_coefficients[step].T, preferred_element_type=F32)
        dims = (((0,), (0,)), ((), ()))
        hessian = lax.dot_general(design, weighted, dims, preferred_element_type=F32)
        adjoint = adjoint - RATE * lax.psum(hessian, "row")
    return adjoint, -RATE * accum


def solution(mesh):
    placed = (
        P("row", "inst"),
        P("row", None),
        P(None, "row", None),
        P(None, "inst", None),
        P("inst", None),
    )
    counts = (mesh.shape["row"], mesh.shape["inst"])
    even = counts[1] > 1 and all(n & (n - 1) == 0 for n in counts)
    return jax.shard_map(
        functools.partial(shards, *counts) if even else plain,
        mesh=mesh,
        in_specs=placed,
        out_specs=(P("inst", None), P("row", "inst")),
        check_vma=False,
    )
```

```python
import functools

import jax
import jax.numpy as jnp
from jax import lax
from jax.experimental import pallas as pl
from jax.experimental.pallas import tpu as pltpu
from jax.sharding import PartitionSpec as P

RATE = 2.0
PARTS = 4
F32 = jnp.float32
BF16 = jnp.bfloat16
ANY = pl.BlockSpec(memory_space=pl.ANY)
VMEM = pl.BlockSpec(memory_space=pltpu.VMEM)
FREE = pl.CostEstimate(flops=0, bytes_accessed=0, transcendentals=0)


def span(bit, size):
    return pl.ds(pl.multiple_of(bit * size, size), size)


def near(value):
    return pltpu.with_memory_space_constraint(value, pltpu.VMEM)


def core_bit():
    return lax.rem(lax.axis_index("inst"), 2)


def side_bit():
    place = lax.axis_index("row")
    return lax.rem(place + lax.div(place, 2), 2)


def call(body, outs, *operands, name, scratch=(), limit=12):
    return pl.pallas_call(
        body,
        in_specs=[VMEM] * len(operands),
        out_specs=[VMEM] * len(outs),
        out_shape=[pltpu.VMEM(shape, dtype) for shape, dtype in outs],
        scratch_shapes=[pltpu.VMEM(shape, dtype) for shape, dtype in scratch],
        compiler_params=pltpu.CompilerParams(vmem_limit_bytes=limit << 20),
        cost_estimate=FREE,
        name=name,
    )(*[near(v) for v in operands])


def prepare_kernel(logits, labels, residual, *curvatures):
    probability = jax.nn.sigmoid(logits[0])
    residual[...] = (probability - labels[...].astype(F32)).astype(BF16)
    cols = curvatures[0].shape[1]
    for c, curvature in enumerate(curvatures):
        mine = probability[:, c * cols : (c + 1) * cols]
        curvature[...] = mine * (1.0 - mine)


def prepare(logits, labels, step):
    _, rows, depth = logits.shape
    block = min(256, rows)
    return pl.pallas_call(
        prepare_kernel,
        grid=(rows // block,),
        in_specs=[
            pl.BlockSpec((1, block, depth), lambda i: (step, i, 0)),
            pl.BlockSpec((block, depth), lambda i: (i, 0)),
        ],
        out_specs=[pl.BlockSpec((block, depth), lambda i: (i, 0))]
        + [pl.BlockSpec((block, depth // 2), lambda i: (i, 0))] * 2,
        out_shape=[jax.ShapeDtypeStruct((rows, depth), BF16)]
        + [jax.ShapeDtypeStruct((rows, depth // 2), F32)] * 2,
        compiler_params=pltpu.CompilerParams(vmem_limit_bytes=12 << 20),
        cost_estimate=FREE,
        name="prepare",
    )(logits, labels)


def part_out(bit, total, kept, sent):
    half = kept.shape[0]
    sent[...] = total[span(1 - bit, half), :].astype(BF16)
    kept[...] = total[span(bit, half), :]


def halve(value, own, other):
    half = own.shape[0]
    own[...] = value[span(side_bit(), half), :].astype(own.dtype)
    other[...] = value[span(1 - side_bit(), half), :].astype(other.dtype)


def first_kernel(blocks, source, start, z, own, other, low_own, low_other, kept, sent, begun, low, total, sems):
    block = z.shape[0] // blocks
    rows = [pl.ds(k * block, block) for k in range(blocks)]
    copies = [
        pltpu.make_async_copy(source.at[r, :], z.at[r, :], sems.at[k]) for k, r in enumerate(rows)
    ]
    opening = pltpu.make_async_copy(start.at[:, : begun.shape[1]], begun, sems.at[blocks])
    opening.start()
    for copy in copies:
        copy.start()
    opening.wait()
    low[...] = begun[...].astype(BF16)
    halve(begun, own, other)
    halve(begun, low_own, low_other)
    for r, copy in zip(rows, copies):
        copy.wait()
        total[r, :] = jnp.dot(z[r, :], low[...], preferred_element_type=F32)
    part_out(core_bit(), total, kept, sent)


def halves(width, cols, *dtypes):
    return [((width // 2, cols), dtype) for dtype in dtypes]


def first_forward(design, start):
    rows, width = design.shape
    cols = start.shape[1] // 2
    blocks = 8
    outs = [((rows, width), BF16)]
    outs += halves(width, cols, F32, F32, BF16, BF16) + halves(rows, cols, F32, BF16)
    return pl.pallas_call(
        functools.partial(first_kernel, blocks),
        in_specs=[pl.BlockSpec(memory_space=pltpu.HBM)] * 2,
        out_specs=[VMEM] * len(outs),
        out_shape=[pltpu.VMEM(shape, dtype) for shape, dtype in outs],
        scratch_shapes=[
            pltpu.VMEM((width, cols), F32),
            pltpu.VMEM((width, cols), BF16),
            pltpu.VMEM((rows, cols), F32),
            pltpu.SemaphoreType.DMA((blocks + 1,)),
        ],
        compiler_params=pltpu.CompilerParams(vmem_limit_bytes=16 << 20),
        cost_estimate=FREE,
        name="first",
    )(*[pltpu.with_memory_space_constraint(v, pltpu.HBM) for v in (design, start)])


def second_kernel(z, start, own, other, low_own, low_other, kept, sent, low, total):
    low[...] = start[...].astype(BF16)
    halve(start, own, other)
    halve(start, low_own, low_other)
    total[...] = jnp.dot(z[...], low[...], preferred_element_type=F32)
    part_out(core_bit(), total, kept, sent)


def second_forward(z, start):
    (rows, width), cols = z.shape, start.shape[1]
    outs = halves(width, cols, F32, F32, BF16, BF16) + halves(rows, cols, F32, BF16)
    scratch = [((width, cols), BF16), ((rows, cols), F32)]
    return call(second_kernel, outs, z, start, name="second", scratch=scratch)


def columns_kernel(start, out):
    out[...] = start[...]


def columns(start, c):
    count, depth = start.shape
    return pl.pallas_call(
        columns_kernel,
        grid=(1,),
        in_specs=[pl.BlockSpec((count, depth // 2), lambda i: (0, c))],
        out_specs=VMEM,
        out_shape=pltpu.VMEM((count, depth // 2), F32),
        compiler_params=pltpu.CompilerParams(vmem_limit_bytes=12 << 20),
        cost_estimate=FREE,
        name="columns",
    )(start)


def early_kernel(z, adjoint, hessian, new, low, partial):
    value = adjoint[...] - RATE * hessian[...].astype(F32)
    new[...] = value
    low[...] = value.astype(BF16)
    partial[...] = jnp.dot(z[:, span(side_bit(), low.shape[0])], low[...], preferred_element_type=F32)


def early(z, adjoint, hessian):
    half, cols = adjoint.shape
    outs = [((half, cols), F32), ((half, cols), BF16), ((z.shape[0], cols), F32)]
    return call(early_kernel, outs, z, adjoint, hessian, name="early")


def late_kernel(z, partial, adjoint, hessian, new, low, sent):
    value = adjoint[...] - RATE * hessian[...].astype(F32)
    new[...] = value
    low[...] = value.astype(BF16)
    rows = span(1 - core_bit(), sent.shape[0])
    cols = span(1 - side_bit(), low.shape[0])
    total = partial[rows, :] + jnp.dot(z[rows, cols], low[...], preferred_element_type=F32)
    sent[...] = total.astype(BF16)


def late(z, partial, adjoint, hessian):
    half, cols = adjoint.shape
    outs = [((half, cols), F32), ((half, cols), BF16), ((z.shape[0] // 2, cols), BF16)]
    return call(late_kernel, outs, z, partial, adjoint, hessian, name="late")


def keep_kernel(z, partial, low, kept):
    rows = span(core_bit(), kept.shape[0])
    cols = span(1 - side_bit(), low.shape[0])
    kept[...] = partial[rows, :] + jnp.dot(z[rows, cols], low[...], preferred_element_type=F32)


def keep(z, partial, low):
    outs = [((z.shape[0] // 2, low.shape[1]), F32)]
    return call(keep_kernel, outs, z, partial, low, name="keep")[0]


def add_kernel(one, two, total, low):
    value = one[...] + two[...].astype(F32)
    total[...] = value
    low[...] = value.astype(BF16)


def add(one, two):
    return call(add_kernel, [(one.shape, F32), (one.shape, BF16)], one, two, name="add")


def weigh_kernel(one, two, curvature, out):
    mine = curvature[span(core_bit(), one.shape[0]), :]
    out[...] = (mine * (one[...] + two[...].astype(F32))).astype(BF16)


def weigh(one, two, curvature):
    return call(weigh_kernel, [(one.shape, BF16)], one, two, curvature, name="weigh")[0]


ROWS = (((0,), (0,)), ((), ()))


def backward_kernel(z, w_own, w_other, weight, sent):
    half = w_own.shape[0]
    weight[span(core_bit(), half), :] = w_own[...]
    weight[span(1 - core_bit(), half), :] = w_other[...]
    cols = span(1 - side_bit(), sent.shape[0])
    total = lax.dot_general(weight[...], z[:, cols], ROWS, preferred_element_type=F32)
    sent[...] = total.T.astype(BF16)


def backward(z, w_own, w_other):
    (rows, width), cols = z.shape, w_own.shape[1]
    outs = [((rows, cols), BF16), ((width // 2, cols), BF16)]
    return call(backward_kernel, outs, z, w_own, w_other, name="backward")


def stay_kernel(z, weight, kept):
    cols = span(side_bit(), kept.shape[0])
    kept[...] = lax.dot_general(weight[...], z[:, cols], ROWS, preferred_element_type=F32).T


def stay(z, weight):
    outs = [((z.shape[1] // 2, weight.shape[1]), F32)]
    return call(stay_kernel, outs, z, weight, name="stay")[0]


def merge_kernel(one, two, out):
    out[...] = (one[...].astype(F32) + two[...].astype(F32)).astype(BF16)


def merge(one, two):
    return call(merge_kernel, [(one.shape, BF16)], one, two, name="merge")[0]


def join_kernel(one, two, out):
    cols = one.shape[1]
    out[:, :cols] = one[...]
    out[:, cols:] = two[...]


def join(pair):
    shape = (pair[0].shape[0], 2 * pair[0].shape[1])
    return call(join_kernel, [(shape, BF16)], *pair, name="join")[0]


def place_kernel(*refs):
    out, half = refs[-1], refs[0].shape[0]
    cols = refs[0].shape[1]
    for k, ref in enumerate(refs[:-1]):
        bit = side_bit() if k % 2 == 0 else 1 - side_bit()
        out[span(bit, half), k // 2 * cols : (k // 2 + 1) * cols] = ref[...]


def place(lows):
    half, cols = lows[0].shape
    return call(place_kernel, [((2 * half, cols * len(lows) // 2), BF16)], *lows, name="place")[0]


def finish_kernel(own, other, hess_own, hess_other, *refs):
    out, half = refs[-1], own.shape[0]
    for bit, a, h in ((side_bit(), own, hess_own), (1 - side_bit(), other, hess_other)):
        out[span(bit, half), :] = a[...] - RATE * h[...].astype(F32)


def finish(adjoint, hessian, c, held):
    half, cols = adjoint[0].shape
    return pl.pallas_call(
        finish_kernel,
        grid=(1,),
        in_specs=[VMEM] * 4 + [ANY for _ in held],
        out_specs=pl.BlockSpec((2 * half, cols), lambda i: (0, c)),
        out_shape=jax.ShapeDtypeStruct((2 * half, 2 * cols), F32),
        input_output_aliases={4: 0} if held else {},
        compiler_params=pltpu.CompilerParams(vmem_limit_bytes=12 << 20),
        cost_estimate=FREE,
        name="finish",
    )(*[near(v) for v in (*adjoint, *hessian)], *held)


def outer_kernel(steps, *refs):
    residuals, weights, lows = refs[:steps], refs[steps : 2 * steps], refs[2 * steps : 3 * steps]
    coefficients, out = refs[3 * steps], refs[-1]
    dims = (((1,), (1,)), ((), ()))
    pairs = [(r[...], b[...]) for r, b in zip(residuals, lows)]
    pairs += [(w[...], coefficients[steps - 1 - k]) for k, w in enumerate(weights)]
    total = lax.dot_general(*pairs[0], dims, preferred_element_type=F32)
    for a, b in pairs[1:]:
        total += lax.dot_general(a, b, dims, preferred_element_type=F32)
    out[...] = -RATE * total


def outer(residuals, weights, lows, coefficients, part, held):
    rows, depth = residuals[0].shape
    steps, cols = coefficients.shape[:2]
    block = min(256, rows // PARTS)
    count = rows // PARTS // block
    first = part * count
    left = [*residuals, *weights]
    return pl.pallas_call(
        functools.partial(outer_kernel, steps),
        grid=(count,),
        in_specs=[pl.BlockSpec((block, depth), lambda i: (first + i, 0)) for _ in left]
        + [VMEM] * (steps + 1)
        + [ANY for _ in held],
        out_specs=pl.BlockSpec((block, cols), lambda i: (first + i, 0)),
        out_shape=jax.ShapeDtypeStruct((rows, cols), F32),
        input_output_aliases={3 * steps + 1: 0} if held else {},
        compiler_params=pltpu.CompilerParams(vmem_limit_bytes=14 << 20),
        cost_estimate=FREE,
        name="outer",
    )(*left, *[near(v) for v in (*lows, coefficients)], *held)


def swap(value, axis, count, bit):
    return lax.ppermute(value, axis, [(i, i ^ bit) for i in range(count)])


class Turn:
    def __init__(self):
        self.last = ()

    def begin(self, *values):
        return lax.optimization_barrier((*values, *self.last))[: len(values)]

    def end(self, value):
        self.last = (value,)


def chain(turn, counts, design, z, curvature, adjoint, steps):
    rows_count, inst_count = counts
    crossings = [1 << b for b in range(1, inst_count.bit_length() - 1)]
    mirrors = [(2 << b) - 1 for b in range(1, rows_count.bit_length() - 1)]
    for step in range(steps - 1, -1, -1):
        if step == steps - 1:
            (adjoint,) = turn.begin(adjoint)
            if z is None:
                z, *out = first_forward(design, adjoint)
            else:
                out = second_forward(z, adjoint)
            *adjoint, low_own, low_other, product, sent = out
            sent = swap(sent, "inst", inst_count, 1)
        else:
            (other,) = turn.begin(hessian[1])
            adjoint[1], low_other, sent = late(z, partial, adjoint[1], other)
            sent = swap(sent, "inst", inst_count, 1)
            product = keep(z, partial, low_other)
        turn.end(product)
        yield "V", (low_own, low_other), z
        for k in range(len(crossings)):
            product, sent = turn.begin(product, sent)
            product, moved = add(product, sent)
            turn.end(moved)
            bits = (crossings[k], crossings[(k + 1) % len(crossings)])
            sent = lax.ppermute(moved, "inst", [(i, i ^ bits[i & 1]) for i in range(inst_count)])
            yield f"x{k}", None
        product, sent = turn.begin(product, sent)
        w_own = weigh(product, sent, curvature[step])
        turn.end(w_own)
        w_other = swap(w_own, "inst", inst_count, 1)
        yield "W", None
        w_own, w_other = turn.begin(w_own, w_other)
        weight, sent = backward(z, w_own, w_other)
        if rows_count > 1:
            sent = swap(sent, "row", rows_count, 1)
        total = stay(z, weight)
        turn.end(total)
        yield "H", weight
        if rows_count > 1:
            for k in range(len(mirrors) + 1):
                total, sent = turn.begin(total, sent)
                total = merge(total, sent)
                turn.end(total)
                sent = swap(total, "row", rows_count, (mirrors + [1])[k])
                yield f"z{k}", None
        hessian = (total, sent)
        if step:
            (total,) = turn.begin(total)
            adjoint[0], low_own, partial = early(z, adjoint[0], total)
            turn.end(partial)
            yield "E", None
    yield "end", adjoint, hessian


def shards(rows_count, inst_count, design, labels, saved_logits, saved_coefficients, cotangent):
    steps = saved_logits.shape[0]
    turn = Turn()
    prepared = [None] * steps
    curvatures = [[None] * steps for _ in range(2)]

    def ready(step, labels):
        prepared[step], curvatures[0][step], curvatures[1][step] = prepare(saved_logits, labels, step)

    ready(steps - 1, labels)
    counts = (rows_count, inst_count)
    chains = [chain(turn, counts, design, None, curvatures[0], cotangent, steps), None]
    lows, weights = [], []

    def joined(how, *values):
        (one,) = turn.begin(values[0])
        out = how((one, *values[1:]))
        turn.end(out)
        return out

    parts, grad, first = 0, (), ()
    crossings = max(rows_count.bit_length() - 1, 0)
    second = columns(cotangent, 1)
    for c in turns(steps, max(inst_count.bit_length() - 2, 0), crossings):
        if c and chains[1] is None:
            chains[1] = chain(turn, counts, design, z, curvatures[1], second, steps)
        stage, *values = next(chains[c])
        if stage == "V" and c:
            lows.append((*seen, *values[0]))
        elif stage == "V":
            seen, z = values
        elif stage == "H" and c:
            weights.append((held, values[0]))
            lows[-1], weights[-1] = joined(place, *lows[-1]), joined(join, *weights[-1])
            if len(weights) < steps:
                ready(steps - 1 - len(weights), turn.begin(labels)[0])
                turn.end(curvatures[0][steps - 1 - len(weights)])
        elif stage == "H":
            held = values[0]
        for _ in range({"H": 1, "z0": 2}.get(stage, 0) if c and len(weights) == steps else 0):
            grad = part_of(turn, prepared[::-1], weights, lows, saved_coefficients, parts, grad)
            parts += 1
    for c in range(2):
        _, adjoint, hessian = next(chains[c])
        while c and parts < PARTS:
            grad = part_of(turn, prepared[::-1], weights, lows, saved_coefficients, parts, grad)
            parts += 1
        hessian = turn.begin(*hessian)
        first = (finish(adjoint, hessian, c, first),)
        turn.end(first[0])
    return first[0], grad[0]


def part_of(turn, residuals, weights, lows, coefficients, part, grad):
    low, *rest = turn.begin(lows[0], *lows[1:])
    grad = (outer(residuals, weights, [low, *rest], coefficients, part, grad),)
    turn.end(grad[0])
    return grad


def turns(steps, crossings, hops):
    order = []
    for step in range(steps):
        order += [0] + [1] * (min(hops, 1) if step else 0)
        order += [0] * min(crossings, 1) + [1] * (1 if step else 0)
        order += [0] * max(crossings - 1, 0) + [1]
        order += [0] + [1] * min(crossings, 1)
        order += [0] + [1] * max(crossings - 1, 0)
        order += [0] * min(hops, 1) + [1, 1]
        order += ([0] + [1]) * max(hops - 1, 0)
        order += [0] * (1 if step < steps - 1 else 0)
    return order + [1] * min(hops, 1)


def plain(design, labels, saved_logits, saved_coefficients, cotangent):
    adjoint = cotangent
    accum = jnp.zeros(design.shape, F32)
    targets = labels.astype(F32)
    for step in range(saved_logits.shape[0] - 1, -1, -1):
        low = adjoint.astype(BF16)
        product = lax.psum(jnp.dot(design, low, preferred_element_type=F32), "inst")
        probability = jax.nn.sigmoid(saved_logits[step])
        residual = (probability - targets).astype(BF16)
        weighted = (probability * (1.0 - probability) * product).astype(BF16)
        accum = accum + jnp.dot(residual, low.T, preferred_element_type=F32)
        accum = accum + jnp.dot(weighted, saved_coefficients[step].T, preferred_element_type=F32)
        dims = (((0,), (0,)), ((), ()))
        hessian = lax.dot_general(design, weighted, dims, preferred_element_type=F32)
        adjoint = adjoint - RATE * lax.psum(hessian, "row")
    return adjoint, -RATE * accum


def solution(mesh):
    placed = (
        P("row", "inst"),
        P("row", None),
        P(None, "row", None),
        P(None, "inst", None),
        P("inst", None),
    )
    counts = (mesh.shape["row"], mesh.shape["inst"])
    even = counts[1] > 1 and all(n & (n - 1) == 0 for n in counts)
    return jax.shard_map(
        functools.partial(shards, *counts) if even else plain,
        mesh=mesh,
        in_specs=placed,
        out_specs=(P("inst", None), P("row", "inst")),
        check_vma=False,
    )
```

```python
import functools

import jax
import jax.numpy as jnp
from jax import lax
from jax.experimental import pallas as pl
from jax.experimental.pallas import tpu as pltpu
from jax.sharding import PartitionSpec as P

RATE = 2.0
PARTS = 4
F32 = jnp.float32
BF16 = jnp.bfloat16
ANY = pl.BlockSpec(memory_space=pl.ANY)
VMEM = pl.BlockSpec(memory_space=pltpu.VMEM)
FREE = pl.CostEstimate(flops=0, bytes_accessed=0, transcendentals=0)


def span(bit, size):
    return pl.ds(pl.multiple_of(bit * size, size), size)


def near(value):
    return pltpu.with_memory_space_constraint(value, pltpu.VMEM)


def core_bit():
    return lax.rem(lax.axis_index("inst"), 2)


def side_bit():
    place = lax.axis_index("row")
    return lax.rem(place + lax.div(place, 2), 2)


def call(body, outs, *operands, name, scratch=(), limit=12):
    return pl.pallas_call(
        body,
        in_specs=[VMEM] * len(operands),
        out_specs=[VMEM] * len(outs),
        out_shape=[pltpu.VMEM(shape, dtype) for shape, dtype in outs],
        scratch_shapes=[pltpu.VMEM(shape, dtype) for shape, dtype in scratch],
        compiler_params=pltpu.CompilerParams(vmem_limit_bytes=limit << 20),
        cost_estimate=FREE,
        name=name,
    )(*[near(v) for v in operands])


def prepare_kernel(logits, labels, residual, *curvatures):
    probability = jax.nn.sigmoid(logits[0])
    residual[...] = (probability - labels[...].astype(F32)).astype(BF16)
    cols = curvatures[0].shape[1]
    for c, curvature in enumerate(curvatures):
        mine = probability[:, c * cols : (c + 1) * cols]
        curvature[...] = mine * (1.0 - mine)


def prepare(logits, labels, step):
    _, rows, depth = logits.shape
    block = min(256, rows)
    return pl.pallas_call(
        prepare_kernel,
        grid=(rows // block,),
        in_specs=[
            pl.BlockSpec((1, block, depth), lambda i: (step, i, 0)),
            pl.BlockSpec((block, depth), lambda i: (i, 0)),
        ],
        out_specs=[pl.BlockSpec((block, depth), lambda i: (i, 0))]
        + [pl.BlockSpec((block, depth // 2), lambda i: (i, 0))] * 2,
        out_shape=[jax.ShapeDtypeStruct((rows, depth), BF16)]
        + [jax.ShapeDtypeStruct((rows, depth // 2), F32)] * 2,
        compiler_params=pltpu.CompilerParams(vmem_limit_bytes=12 << 20),
        cost_estimate=FREE,
        name="prepare",
    )(logits, labels)


def part_out(bit, total, kept, sent):
    half = kept.shape[0]
    sent[...] = total[span(1 - bit, half), :].astype(BF16)
    kept[...] = total[span(bit, half), :]


def first_kernel(blocks, source, start, z, adjoint, low, kept, sent, total, sems):
    block = z.shape[0] // blocks
    rows = [pl.ds(k * block, block) for k in range(blocks)]
    copies = [
        pltpu.make_async_copy(source.at[r, :], z.at[r, :], sems.at[k]) for k, r in enumerate(rows)
    ]
    for copy in copies:
        copy.start()
    adjoint[...] = start[...]
    low[...] = start[...].astype(BF16)
    for r, copy in zip(rows, copies):
        copy.wait()
        total[r, :] = jnp.dot(z[r, :], low[...], preferred_element_type=F32)
    part_out(core_bit(), total, kept, sent)


def first_forward(design, start):
    rows, width = design.shape
    cols = start.shape[1] // 2
    blocks = 8
    outs = [((rows, width), BF16), ((width, cols), F32), ((width, cols), BF16)]
    outs += [((rows // 2, cols), F32), ((rows // 2, cols), BF16)]
    return pl.pallas_call(
        functools.partial(first_kernel, blocks),
        grid=(1,),
        in_specs=[
            pl.BlockSpec(memory_space=pltpu.HBM),
            pl.BlockSpec((width, cols), lambda i: (0, 0)),
        ],
        out_specs=[VMEM] * len(outs),
        out_shape=[pltpu.VMEM(shape, dtype) for shape, dtype in outs],
        scratch_shapes=[pltpu.VMEM((rows, cols), F32), pltpu.SemaphoreType.DMA((blocks,))],
        compiler_params=pltpu.CompilerParams(vmem_limit_bytes=16 << 20),
        cost_estimate=FREE,
        name="first",
    )(pltpu.with_memory_space_constraint(design, pltpu.HBM), start)


def columns_kernel(start, out):
    out[...] = start[...]


def columns(start, c):
    count, depth = start.shape
    return pl.pallas_call(
        columns_kernel,
        grid=(1,),
        in_specs=[pl.BlockSpec((count, depth // 2), lambda i: (0, c))],
        out_specs=VMEM,
        out_shape=pltpu.VMEM((count, depth // 2), F32),
        compiler_params=pltpu.CompilerParams(vmem_limit_bytes=12 << 20),
        cost_estimate=FREE,
        name="columns",
    )(start)


def forward_kernel(updates, z, adjoint, *refs):
    hessian, (*new, low, kept, sent, total) = refs[:updates], refs[updates:]
    if updates:
        half = hessian[0].shape[0]
        for bit, h in zip((side_bit(), 1 - side_bit()), hessian):
            rows = span(bit, half)
            value = adjoint[rows, :] - RATE * h[...].astype(F32)
            new[0][rows, :] = value
            low[rows, :] = value.astype(BF16)
    else:
        low[...] = adjoint[...].astype(BF16)
    total[...] = jnp.dot(z[...], low[...], preferred_element_type=F32)
    part_out(core_bit(), total, kept, sent)


def forward(z, adjoint, hessian):
    (rows, width), cols = z.shape, adjoint.shape[1]
    outs = [((width, cols), F32)] if hessian else []
    outs += [((width, cols), BF16), ((rows // 2, cols), F32), ((rows // 2, cols), BF16)]
    body = functools.partial(forward_kernel, len(hessian))
    out = call(body, outs, z, adjoint, *hessian, name="forward", scratch=[((rows, cols), F32)])
    return out if hessian else [adjoint, *out]


def add_kernel(one, two, total, low):
    value = one[...] + two[...].astype(F32)
    total[...] = value
    low[...] = value.astype(BF16)


def add(one, two):
    return call(add_kernel, [(one.shape, F32), (one.shape, BF16)], one, two, name="add")


def weigh_kernel(one, two, curvature, out):
    mine = curvature[span(core_bit(), one.shape[0]), :]
    out[...] = (mine * (one[...] + two[...].astype(F32))).astype(BF16)


def weigh(one, two, curvature):
    return call(weigh_kernel, [(one.shape, BF16)], one, two, curvature, name="weigh")[0]


def backward_kernel(z, w_own, w_other, weight, kept, sent, total):
    half = w_own.shape[0]
    weight[span(core_bit(), half), :] = w_own[...]
    weight[span(1 - core_bit(), half), :] = w_other[...]
    dims = (((0,), (0,)), ((), ()))
    total[...] = lax.dot_general(weight[...], z[...], dims, preferred_element_type=F32).T
    part_out(side_bit(), total, kept, sent)


def backward(z, w_own, w_other):
    (rows, width), cols = z.shape, w_own.shape[1]
    outs = [((rows, cols), BF16), ((width // 2, cols), F32), ((width // 2, cols), BF16)]
    return call(
        backward_kernel, outs, z, w_own, w_other, name="backward", scratch=[((width, cols), F32)]
    )


def merge_kernel(one, two, out):
    out[...] = (one[...].astype(F32) + two[...].astype(F32)).astype(BF16)


def merge(one, two):
    return call(merge_kernel, [(one.shape, BF16)], one, two, name="merge")[0]


def join_kernel(one, two, out):
    cols = one.shape[1]
    out[:, :cols] = one[...]
    out[:, cols:] = two[...]


def join(one, two):
    return call(join_kernel, [((one.shape[0], 2 * one.shape[1]), BF16)], one, two, name="join")[0]


def finish_kernel(adjoint, own, other, *refs):
    out, half = refs[-1], own.shape[0]
    for bit, h in zip((side_bit(), 1 - side_bit()), (own, other)):
        rows = span(bit, half)
        out[rows, :] = adjoint[rows, :] - RATE * h[...].astype(F32)


def finish(adjoint, hessian, c, held):
    count, cols = adjoint.shape
    return pl.pallas_call(
        finish_kernel,
        grid=(1,),
        in_specs=[VMEM, VMEM, VMEM] + [ANY for _ in held],
        out_specs=pl.BlockSpec((count, cols), lambda i: (0, c)),
        out_shape=jax.ShapeDtypeStruct((count, 2 * cols), F32),
        input_output_aliases={3: 0} if held else {},
        compiler_params=pltpu.CompilerParams(vmem_limit_bytes=12 << 20),
        cost_estimate=FREE,
        name="finish",
    )(*[near(v) for v in (adjoint, *hessian)], *held)


def outer_kernel(steps, *refs):
    residuals, weights, lows = refs[:steps], refs[steps : 2 * steps], refs[2 * steps : 3 * steps]
    coefficients, out = refs[3 * steps], refs[-1]
    dims = (((1,), (1,)), ((), ()))
    pairs = [(r[...], b[...]) for r, b in zip(residuals, lows)]
    pairs += [(w[...], coefficients[steps - 1 - k]) for k, w in enumerate(weights)]
    total = lax.dot_general(*pairs[0], dims, preferred_element_type=F32)
    for a, b in pairs[1:]:
        total += lax.dot_general(a, b, dims, preferred_element_type=F32)
    out[...] = -RATE * total


def outer(residuals, weights, lows, coefficients, part, held):
    rows, depth = residuals[0].shape
    steps, cols = coefficients.shape[:2]
    block = min(256, rows // PARTS)
    count = rows // PARTS // block
    first = part * count
    left = [*residuals, *weights]
    return pl.pallas_call(
        functools.partial(outer_kernel, steps),
        grid=(count,),
        in_specs=[pl.BlockSpec((block, depth), lambda i: (first + i, 0)) for _ in left]
        + [VMEM] * (steps + 1)
        + [ANY for _ in held],
        out_specs=pl.BlockSpec((block, cols), lambda i: (first + i, 0)),
        out_shape=jax.ShapeDtypeStruct((rows, cols), F32),
        input_output_aliases={3 * steps + 1: 0} if held else {},
        compiler_params=pltpu.CompilerParams(vmem_limit_bytes=14 << 20),
        cost_estimate=FREE,
        name="outer",
    )(*left, *[near(v) for v in (*lows, coefficients)], *held)


def swap(value, axis, count, bit):
    return lax.ppermute(value, axis, [(i, i ^ bit) for i in range(count)])


class Turn:
    def __init__(self):
        self.last = ()

    def begin(self, *values):
        return lax.optimization_barrier((*values, *self.last))[: len(values)]

    def end(self, value):
        self.last = (value,)


def chain(turn, counts, design, z, curvature, adjoint, steps):
    rows_count, inst_count = counts
    crossings = [1 << b for b in range(1, inst_count.bit_length() - 1)]
    mirrors = [(2 << b) - 1 for b in range(1, rows_count.bit_length() - 1)]
    hessian = ()
    for step in range(steps - 1, -1, -1):
        adjoint, *hessian = turn.begin(adjoint, *hessian)
        if z is None:
            z, adjoint, low, product, sent = first_forward(design, adjoint)
        else:
            adjoint, low, product, sent = forward(z, adjoint, hessian)
        turn.end(product)
        sent = swap(sent, "inst", inst_count, 1)
        yield "V", low, z
        for k in range(len(crossings)):
            product, sent = turn.begin(product, sent)
            product, moved = add(product, sent)
            turn.end(moved)
            bits = (crossings[k], crossings[(k + 1) % len(crossings)])
            sent = lax.ppermute(moved, "inst", [(i, i ^ bits[i & 1]) for i in range(inst_count)])
            yield f"x{k}", None
        product, sent = turn.begin(product, sent)
        w_own = weigh(product, sent, curvature[step])
        turn.end(w_own)
        w_other = swap(w_own, "inst", inst_count, 1)
        yield "W", None
        w_own, w_other = turn.begin(w_own, w_other)
        weight, total, sent = backward(z, w_own, w_other)
        turn.end(total)
        if rows_count > 1:
            sent = swap(sent, "row", rows_count, 1)
        yield "H", weight
        if rows_count > 1:
            for k in range(len(mirrors) + 1):
                total, sent = turn.begin(total, sent)
                total = merge(total, sent)
                turn.end(total)
                sent = swap(total, "row", rows_count, (mirrors + [1])[k])
                yield f"z{k}", None
        hessian = (total, sent)
    yield "end", adjoint, hessian


def shards(rows_count, inst_count, design, labels, saved_logits, saved_coefficients, cotangent):
    steps = saved_logits.shape[0]
    turn = Turn()
    prepared = [prepare(saved_logits, labels, step) for step in range(steps)]
    residuals = [p[0] for p in prepared[::-1]]
    curvatures = [[p[1 + c] for p in prepared] for c in range(2)]
    counts = (rows_count, inst_count)
    chains = [chain(turn, counts, design, None, curvatures[0], cotangent, steps), None]
    lows, weights = [], []

    def joined(value):
        (one,) = turn.begin(value[0])
        out = join(one, value[1])
        turn.end(out)
        return out

    parts, grad, first = 0, (), ()
    crossings = max(rows_count.bit_length() - 1, 0)
    second = columns(cotangent, 1)
    for c in turns(steps, max(inst_count.bit_length() - 2, 0), crossings):
        if c and chains[1] is None:
            chains[1] = chain(turn, counts, design, z, curvatures[1], second, steps)
        stage, *values = next(chains[c])
        if stage == "V" and c:
            lows.append((seen, values[0]))
        elif stage == "V":
            seen, z = values
        elif stage == "H" and c:
            weights.append((held, values[0]))
            lows[-1], weights[-1] = joined(lows[-1]), joined(weights[-1])
        elif stage == "H":
            held = values[0]
        for _ in range({"H": 1, "z0": 2}.get(stage, 0) if c and len(weights) == steps else 0):
            grad = part_of(turn, residuals, weights, lows, saved_coefficients, parts, grad)
            parts += 1
    for c in range(2):
        _, adjoint, hessian = next(chains[c])
        while c and parts < PARTS:
            grad = part_of(turn, residuals, weights, lows, saved_coefficients, parts, grad)
            parts += 1
        adjoint, *hessian = turn.begin(adjoint, *hessian)
        first = (finish(adjoint, hessian, c, first),)
        turn.end(first[0])
    return first[0], grad[0]


def part_of(turn, residuals, weights, lows, coefficients, part, grad):
    low, *rest = turn.begin(lows[0], *lows[1:])
    grad = (outer(residuals, weights, [low, *rest], coefficients, part, grad),)
    turn.end(grad[0])
    return grad


def turns(steps, crossings, hops):
    order = []
    for step in range(steps):
        order += [0] + [1] * (min(hops, 1) if step else 0)
        order += [0] * crossings + [1]
        order += [0] + [1] * min(crossings, 1)
        order += [0] + [1] * max(crossings - 1, 0)
        order += [0] * min(hops, 1) + [1, 1]
        order += ([0] + [1]) * max(hops - 1, 0)
    return order + [1] * min(hops, 1)


def plain(design, labels, saved_logits, saved_coefficients, cotangent):
    adjoint = cotangent
    accum = jnp.zeros(design.shape, F32)
    targets = labels.astype(F32)
    for step in range(saved_logits.shape[0] - 1, -1, -1):
        low = adjoint.astype(BF16)
        product = lax.psum(jnp.dot(design, low, preferred_element_type=F32), "inst")
        probability = jax.nn.sigmoid(saved_logits[step])
        residual = (probability - targets).astype(BF16)
        weighted = (probability * (1.0 - probability) * product).astype(BF16)
        accum = accum + jnp.dot(residual, low.T, preferred_element_type=F32)
        accum = accum + jnp.dot(weighted, saved_coefficients[step].T, preferred_element_type=F32)
        dims = (((0,), (0,)), ((), ()))
        hessian = lax.dot_general(design, weighted, dims, preferred_element_type=F32)
        adjoint = adjoint - RATE * lax.psum(hessian, "row")
    return adjoint, -RATE * accum


def solution(mesh):
    placed = (
        P("row", "inst"),
        P("row", None),
        P(None, "row", None),
        P(None, "inst", None),
        P("inst", None),
    )
    counts = (mesh.shape["row"], mesh.shape["inst"])
    even = counts[1] > 1 and all(n & (n - 1) == 0 for n in counts)
    return jax.shard_map(
        functools.partial(shards, *counts) if even else plain,
        mesh=mesh,
        in_specs=placed,
        out_specs=(P("inst", None), P("row", "inst")),
        check_vma=False,
    )
```

```python
import functools

import jax
import jax.numpy as jnp
from jax import lax
from jax.experimental import pallas as pl
from jax.experimental.pallas import tpu as pltpu
from jax.sharding import PartitionSpec as P

RATE = 2.0
PARTS = 4
F32 = jnp.float32
BF16 = jnp.bfloat16
ANY = pl.BlockSpec(memory_space=pl.ANY)
VMEM = pl.BlockSpec(memory_space=pltpu.VMEM)
FREE = pl.CostEstimate(flops=0, bytes_accessed=0, transcendentals=0)


def near(value):
    return pltpu.with_memory_space_constraint(value, pltpu.VMEM)


def place_bits():
    core = lax.rem(lax.axis_index("inst"), 2)
    row = lax.axis_index("row")
    side = lax.rem(row + lax.div(row, 2), 2)
    return jnp.concatenate([jnp.full((8, 128), core), jnp.full((8, 128), side)], axis=0)


def pick(bits, which, one, two):
    return jnp.where(bits[8 * which : 8 * which + 1, :] == 0, one, two)


def call(body, outs, *operands, name, scratch=(), limit=12):
    return pl.pallas_call(
        body,
        in_specs=[VMEM] * len(operands),
        out_specs=[VMEM] * len(outs),
        out_shape=[pltpu.VMEM(shape, dtype) for shape, dtype in outs],
        scratch_shapes=[pltpu.VMEM(shape, dtype) for shape, dtype in scratch],
        compiler_params=pltpu.CompilerParams(vmem_limit_bytes=limit << 20),
        cost_estimate=FREE,
        name=name,
    )(*[near(v) for v in operands])


def prepare_kernel(logits, labels, residual, *curvatures):
    probability = jax.nn.sigmoid(logits[0])
    residual[...] = (probability - labels[...].astype(F32)).astype(BF16)
    cols = curvatures[0].shape[1]
    for c, curvature in enumerate(curvatures):
        mine = probability[:, c * cols : (c + 1) * cols]
        curvature[...] = mine * (1.0 - mine)


def prepare(logits, labels, step):
    _, rows, depth = logits.shape
    block = min(256, rows)
    return pl.pallas_call(
        prepare_kernel,
        grid=(rows // block,),
        in_specs=[
            pl.BlockSpec((1, block, depth), lambda i: (step, i, 0)),
            pl.BlockSpec((block, depth), lambda i: (i, 0)),
        ],
        out_specs=[pl.BlockSpec((block, depth), lambda i: (i, 0))]
        + [pl.BlockSpec((block, depth // 2), lambda i: (i, 0))] * 2,
        out_shape=[jax.ShapeDtypeStruct((rows, depth), BF16)]
        + [jax.ShapeDtypeStruct((rows, depth // 2), F32)] * 2,
        compiler_params=pltpu.CompilerParams(vmem_limit_bytes=12 << 20),
        cost_estimate=FREE,
        name="prepare",
    )(logits, labels)


def part_out(bits, which, total, kept, sent):
    half = kept.shape[0]
    sent[...] = pick(bits, which, total[half:, :], total[:half, :]).astype(BF16)
    kept[...] = pick(bits, which, total[:half, :], total[half:, :])


def first_kernel(blocks, bits, source, start, z, adjoint, low, kept, sent, total, sems):
    block = z.shape[0] // blocks
    rows = [pl.ds(k * block, block) for k in range(blocks)]
    copies = [
        pltpu.make_async_copy(source.at[r, :], z.at[r, :], sems.at[k]) for k, r in enumerate(rows)
    ]
    for copy in copies:
        copy.start()
    adjoint[...] = start[...]
    low[...] = start[...].astype(BF16)
    for r, copy in zip(rows, copies):
        copy.wait()
        total[r, :] = jnp.dot(z[r, :], low[...], preferred_element_type=F32)
    part_out(bits, 0, total, kept, sent)


def first_forward(bits, design, start):
    rows, width = design.shape
    cols = start.shape[1] // 2
    blocks = 8
    outs = [((rows, width), BF16), ((width, cols), F32), ((width, cols), BF16)]
    outs += [((rows // 2, cols), F32), ((rows // 2, cols), BF16)]
    return pl.pallas_call(
        functools.partial(first_kernel, blocks),
        grid=(1,),
        in_specs=[
            VMEM,
            pl.BlockSpec(memory_space=pltpu.HBM),
            pl.BlockSpec((width, cols), lambda i: (0, 0)),
        ],
        out_specs=[VMEM] * len(outs),
        out_shape=[pltpu.VMEM(shape, dtype) for shape, dtype in outs],
        scratch_shapes=[pltpu.VMEM((rows, cols), F32), pltpu.SemaphoreType.DMA((blocks,))],
        compiler_params=pltpu.CompilerParams(vmem_limit_bytes=16 << 20),
        cost_estimate=FREE,
        name="first",
    )(near(bits), pltpu.with_memory_space_constraint(design, pltpu.HBM), start)


def columns_kernel(start, out):
    out[...] = start[...]


def columns(start, c):
    count, depth = start.shape
    return pl.pallas_call(
        columns_kernel,
        grid=(1,),
        in_specs=[pl.BlockSpec((count, depth // 2), lambda i: (0, c))],
        out_specs=VMEM,
        out_shape=pltpu.VMEM((count, depth // 2), F32),
        compiler_params=pltpu.CompilerParams(vmem_limit_bytes=12 << 20),
        cost_estimate=FREE,
        name="columns",
    )(start)


def forward_kernel(updates, bits, z, adjoint, *refs):
    hessian, (*new, low, kept, sent, total) = refs[:updates], refs[updates:]
    if updates:
        half = hessian[0].shape[0]
        own, other = (h[...].astype(F32) for h in hessian)
        for k, h in enumerate((pick(bits, 1, own, other), pick(bits, 1, other, own))):
            rows = pl.ds(k * half, half)
            value = adjoint[rows, :] - RATE * h
            new[0][rows, :] = value
            low[rows, :] = value.astype(BF16)
    else:
        low[...] = adjoint[...].astype(BF16)
    total[...] = jnp.dot(z[...], low[...], preferred_element_type=F32)
    part_out(bits, 0, total, kept, sent)


def forward(bits, z, adjoint, hessian):
    (rows, width), cols = z.shape, adjoint.shape[1]
    outs = [((width, cols), F32)] if hessian else []
    outs += [((width, cols), BF16), ((rows // 2, cols), F32), ((rows // 2, cols), BF16)]
    body = functools.partial(forward_kernel, len(hessian))
    out = call(body, outs, bits, z, adjoint, *hessian, name="forward", scratch=[((rows, cols), F32)])
    return out if hessian else [adjoint, *out]


def add_kernel(one, two, total, low):
    value = one[...] + two[...].astype(F32)
    total[...] = value
    low[...] = value.astype(BF16)


def add(one, two):
    return call(add_kernel, [(one.shape, F32), (one.shape, BF16)], one, two, name="add")


def weigh_kernel(bits, one, two, curvature, out):
    half = one.shape[0]
    mine = pick(bits, 0, curvature[:half, :], curvature[half:, :])
    out[...] = (mine * (one[...] + two[...].astype(F32))).astype(BF16)


def weigh(bits, one, two, curvature):
    return call(weigh_kernel, [(one.shape, BF16)], bits, one, two, curvature, name="weigh")[0]


def backward_kernel(bits, z, w_own, w_other, weight, kept, sent, total):
    half = w_own.shape[0]
    own, other = w_own[...].astype(F32), w_other[...].astype(F32)
    weight[:half, :] = pick(bits, 0, own, other).astype(BF16)
    weight[half:, :] = pick(bits, 0, other, own).astype(BF16)
    dims = (((0,), (0,)), ((), ()))
    total[...] = lax.dot_general(weight[...], z[...], dims, preferred_element_type=F32).T
    part_out(bits, 1, total, kept, sent)


def backward(bits, z, w_own, w_other):
    (rows, width), cols = z.shape, w_own.shape[1]
    outs = [((rows, cols), BF16), ((width // 2, cols), F32), ((width // 2, cols), BF16)]
    return call(
        backward_kernel, outs, bits, z, w_own, w_other, name="backward", scratch=[((width, cols), F32)]
    )


def merge_kernel(one, two, out):
    out[...] = (one[...].astype(F32) + two[...].astype(F32)).astype(BF16)


def merge(one, two):
    return call(merge_kernel, [(one.shape, BF16)], one, two, name="merge")[0]


def join_kernel(one, two, out):
    cols = one.shape[1]
    out[:, :cols] = one[...]
    out[:, cols:] = two[...]


def join(one, two):
    return call(join_kernel, [((one.shape[0], 2 * one.shape[1]), BF16)], one, two, name="join")[0]


def finish_kernel(bits, adjoint, own, other, *refs):
    out, half = refs[-1], own.shape[0]
    own, other = own[...].astype(F32), other[...].astype(F32)
    for k, h in enumerate((pick(bits, 1, own, other), pick(bits, 1, other, own))):
        rows = pl.ds(k * half, half)
        out[rows, :] = adjoint[rows, :] - RATE * h


def finish(bits, adjoint, hessian, c, held):
    count, cols = adjoint.shape
    return pl.pallas_call(
        finish_kernel,
        grid=(1,),
        in_specs=[VMEM] * 4 + [ANY for _ in held],
        out_specs=pl.BlockSpec((count, cols), lambda i: (0, c)),
        out_shape=jax.ShapeDtypeStruct((count, 2 * cols), F32),
        input_output_aliases={4: 0} if held else {},
        compiler_params=pltpu.CompilerParams(vmem_limit_bytes=12 << 20),
        cost_estimate=FREE,
        name="finish",
    )(*[near(v) for v in (bits, adjoint, *hessian)], *held)


def outer_kernel(steps, *refs):
    residuals, weights, lows = refs[:steps], refs[steps : 2 * steps], refs[2 * steps : 3 * steps]
    coefficients, out = refs[3 * steps], refs[-1]
    dims = (((1,), (1,)), ((), ()))
    pairs = [(r[...], b[...]) for r, b in zip(residuals, lows)]
    pairs += [(w[...], coefficients[steps - 1 - k]) for k, w in enumerate(weights)]
    total = lax.dot_general(*pairs[0], dims, preferred_element_type=F32)
    for a, b in pairs[1:]:
        total += lax.dot_general(a, b, dims, preferred_element_type=F32)
    out[...] = -RATE * total


def outer(residuals, weights, lows, coefficients, part, held):
    rows, depth = residuals[0].shape
    steps, cols = coefficients.shape[:2]
    block = min(256, rows // PARTS)
    count = rows // PARTS // block
    first = part * count
    left = [*residuals, *weights]
    return pl.pallas_call(
        functools.partial(outer_kernel, steps),
        grid=(count,),
        in_specs=[pl.BlockSpec((block, depth), lambda i: (first + i, 0)) for _ in left]
        + [VMEM] * (steps + 1)
        + [ANY for _ in held],
        out_specs=pl.BlockSpec((block, cols), lambda i: (first + i, 0)),
        out_shape=jax.ShapeDtypeStruct((rows, cols), F32),
        input_output_aliases={3 * steps + 1: 0} if held else {},
        compiler_params=pltpu.CompilerParams(vmem_limit_bytes=14 << 20),
        cost_estimate=FREE,
        name="outer",
    )(*left, *[near(v) for v in (*lows, coefficients)], *held)


def swap(value, axis, count, bit):
    return lax.ppermute(value, axis, [(i, i ^ bit) for i in range(count)])


class Turn:
    def __init__(self):
        self.last = ()

    def begin(self, *values):
        return lax.optimization_barrier((*values, *self.last))[: len(values)]

    def end(self, value):
        self.last = (value,)


def chain(turn, counts, bits, design, z, curvature, adjoint, steps):
    rows_count, inst_count = counts
    crossings = [1 << b for b in range(1, inst_count.bit_length() - 1)]
    mirrors = [(2 << b) - 1 for b in range(1, rows_count.bit_length() - 1)]
    hessian = ()
    for step in range(steps - 1, -1, -1):
        adjoint, *hessian = turn.begin(adjoint, *hessian)
        if z is None:
            z, adjoint, low, product, sent = first_forward(bits, design, adjoint)
        else:
            adjoint, low, product, sent = forward(bits, z, adjoint, hessian)
        turn.end(product)
        sent = swap(sent, "inst", inst_count, 1)
        yield "V", low, z
        for k in range(len(crossings)):
            product, sent = turn.begin(product, sent)
            product, moved = add(product, sent)
            turn.end(moved)
            pair = (crossings[k], crossings[(k + 1) % len(crossings)])
            sent = lax.ppermute(moved, "inst", [(i, i ^ pair[i & 1]) for i in range(inst_count)])
            yield f"x{k}", None
        product, sent = turn.begin(product, sent)
        w_own = weigh(bits, product, sent, curvature[step])
        turn.end(w_own)
        w_other = swap(w_own, "inst", inst_count, 1)
        yield "W", None
        w_own, w_other = turn.begin(w_own, w_other)
        weight, total, sent = backward(bits, z, w_own, w_other)
        turn.end(total)
        if rows_count > 1:
            sent = swap(sent, "row", rows_count, 1)
        yield "H", weight
        if rows_count > 1:
            for k in range(len(mirrors) + 1):
                total, sent = turn.begin(total, sent)
                total = merge(total, sent)
                turn.end(total)
                sent = swap(total, "row", rows_count, (mirrors + [1])[k])
                yield f"z{k}", None
        hessian = (total, sent)
    yield "end", adjoint, hessian


def shards(rows_count, inst_count, design, labels, saved_logits, saved_coefficients, cotangent):
    steps = saved_logits.shape[0]
    bits = place_bits()
    turn = Turn()
    prepared = [prepare(saved_logits, labels, step) for step in range(steps)]
    residuals = [p[0] for p in prepared[::-1]]
    curvatures = [[p[1 + c] for p in prepared] for c in range(2)]
    counts = (rows_count, inst_count)
    chains = [chain(turn, counts, bits, design, None, curvatures[0], cotangent, steps), None]
    lows, weights = [], []

    def joined(value):
        (one,) = turn.begin(value[0])
        out = join(one, value[1])
        turn.end(out)
        return out

    parts, grad, first = 0, (), ()
    crossings = max(rows_count.bit_length() - 1, 0)
    second = columns(cotangent, 1)
    for c in turns(steps, max(inst_count.bit_length() - 2, 0), crossings):
        if c and chains[1] is None:
            chains[1] = chain(turn, counts, bits, design, z, curvatures[1], second, steps)
        stage, *values = next(chains[c])
        if stage == "V" and c:
            lows.append((seen, values[0]))
        elif stage == "V":
            seen, z = values
        elif stage == "H" and c:
            weights.append((held, values[0]))
            lows[-1], weights[-1] = joined(lows[-1]), joined(weights[-1])
        elif stage == "H":
            held = values[0]
        for _ in range({"H": 1, "z0": 2}.get(stage, 0) if c and len(weights) == steps else 0):
            grad = part_of(turn, residuals, weights, lows, saved_coefficients, parts, grad)
            parts += 1
    for c in range(2):
        _, adjoint, hessian = next(chains[c])
        while c and parts < PARTS:
            grad = part_of(turn, residuals, weights, lows, saved_coefficients, parts, grad)
            parts += 1
        adjoint, *hessian = turn.begin(adjoint, *hessian)
        first = (finish(bits, adjoint, hessian, c, first),)
        turn.end(first[0])
    return first[0], grad[0]


def part_of(turn, residuals, weights, lows, coefficients, part, grad):
    low, *rest = turn.begin(lows[0], *lows[1:])
    grad = (outer(residuals, weights, [low, *rest], coefficients, part, grad),)
    turn.end(grad[0])
    return grad


def turns(steps, crossings, hops):
    order = []
    for step in range(steps):
        order += [0] + [1] * (min(hops, 1) if step else 0)
        order += [0] * crossings + [1]
        order += [0] + [1] * min(crossings, 1)
        order += [0] + [1] * max(crossings - 1, 0)
        order += [0] * min(hops, 1) + [1, 1]
        order += ([0] + [1]) * max(hops - 1, 0)
    return order + [1] * min(hops, 1)


def plain(design, labels, saved_logits, saved_coefficients, cotangent):
    adjoint = cotangent
    accum = jnp.zeros(design.shape, F32)
    targets = labels.astype(F32)
    for step in range(saved_logits.shape[0] - 1, -1, -1):
        low = adjoint.astype(BF16)
        product = lax.psum(jnp.dot(design, low, preferred_element_type=F32), "inst")
        probability = jax.nn.sigmoid(saved_logits[step])
        residual = (probability - targets).astype(BF16)
        weighted = (probability * (1.0 - probability) * product).astype(BF16)
        accum = accum + jnp.dot(residual, low.T, preferred_element_type=F32)
        accum = accum + jnp.dot(weighted, saved_coefficients[step].T, preferred_element_type=F32)
        dims = (((0,), (0,)), ((), ()))
        hessian = lax.dot_general(design, weighted, dims, preferred_element_type=F32)
        adjoint = adjoint - RATE * lax.psum(hessian, "row")
    return adjoint, -RATE * accum


def solution(mesh):
    placed = (
        P("row", "inst"),
        P("row", None),
        P(None, "row", None),
        P(None, "inst", None),
        P("inst", None),
    )
    counts = (mesh.shape["row"], mesh.shape["inst"])
    even = counts[1] > 1 and all(n & (n - 1) == 0 for n in counts)
    return jax.shard_map(
        functools.partial(shards, *counts) if even else plain,
        mesh=mesh,
        in_specs=placed,
        out_specs=(P("inst", None), P("row", "inst")),
        check_vma=False,
    )
```
